256 devices in a mesh: dp: 16 (over z_hi, y), shard: 16 (over x, z_lo, core).
Axes of the slice: x: 4, y: 4, z: 8 (z_hi: 4, z_lo: 2; z = z_hi * 2 + z_lo), core: 2. Of those that a mesh axis runs over, the one named last changes fastest.
Arguments:
- tokens: bfloat16 [6144, 2048], P('dp', 'shard'), may hold values from -6 to 6
- cotangent: bfloat16 [6144, 2048], P('dp', 'shard'), may hold values from -6 to 6
- route_probs: float32 [6144], P('dp'), may hold values from 0.2 to 1
- w_gate: bfloat16 [2, 2048, 8192], P(None, 'dp', 'shard'), may hold values from -0.125 to 0.125
- w_up: bfloat16 [2, 2048, 8192], P(None, 'dp', 'shard'), may hold values from -0.125 to 0.125
- w_down: bfloat16 [2, 8192, 2048], P(None, 'shard', 'dp'), may hold values from -0.0625 to 0.0625
- tile_counts: int32 [16, 2], P('dp'), may hold values from 0 to 3, as said below
Outputs:
- layer_out: bfloat16 [6144, 2048], P('dp', 'shard')
- prob_grad: float32 [6144], P('dp')
- input_grad: bfloat16 [6144, 2048], P('dp', 'shard')
- gate_grad: bfloat16 [2, 2048, 8192], P(None, 'dp', 'shard')
- up_grad: bfloat16 [2, 2048, 8192], P(None, 'dp', 'shard')
- down_grad: bfloat16 [2, 8192, 2048], P(None, 'shard', 'dp')
The draws below stay inside these ranges and needn't reach their ends.
Inputs may be any that keep to these rules, and one draw needn't show every extreme that they name: `tile_counts`: each group's counts sum to at most 3 and at least 1; in every draw some group has all 3 slots of one expert.
All inputs are finite; a program needn't handle non-finite values.
Results may differ from the reference program's by a relative error of at most 0.023.
Values may be sent and summed in bfloat16 or wider, within the bound.
No kernel may reach another device: no remote copies, remote signals or barrier semaphores. Data moves between devices by JAX's collectives and lax.ppermute only.
A program may use at most 128 MiB of HBM per device.

```python
import math
import jax
import jax.numpy as jnp
from jax import lax

D = 2048
FF = 8192
EXP = 2
TILE = 128
TILES_DEV = 3
TOKENS = 6144
N_DP = 16
N_SHARD = 16


def draw_tile_counts(key, part):
    key = jax.random.fold_in(key, 7)
    key_live, key_full, key_ids, key_only = jax.random.split(key, 4)
    groups = jnp.arange(N_DP, dtype=jnp.int32)
    live_slots = jax.random.randint(key_live, (N_DP,), 1, TILES_DEV + 1)
    full_group = jax.random.randint(key_full, (), 0, N_DP)
    live_slots = jnp.where(groups == full_group, TILES_DEV, live_slots)
    slot_ids = jax.random.randint(key_ids, (N_DP, TILES_DEV), 0, EXP)
    only_expert = jax.random.randint(key_only, (), 0, EXP)
    slot_ids = jnp.where((groups == full_group)[:, None], only_expert, slot_ids)
    position = jnp.arange(TILES_DEV, dtype=jnp.int32)
    used = position[None, :] < live_slots[:, None]
    onehot = (slot_ids[:, :, None] == jnp.arange(EXP, dtype=jnp.int32)[None, None, :]) & used[:, :, None]
    return jnp.sum(onehot.astype(jnp.int32), axis=1).astype(jnp.int32)


def with_spikes(values, own_key, source, target, parts, factor):
    def block_of(dim):
        return (jnp.arange(values.shape[dim]) // (values.shape[dim] // parts)).reshape((-1,) + (1,) * (values.ndim - 1 - dim))

    one_side = jax.random.permutation(own_key, parts)[block_of(target)]
    other_side = (block_of(target) + parts // 2) % parts
    return jnp.where((block_of(source) == one_side) | (block_of(source) == other_side), factor * values, values)


def steps_of(stream_key, extent, cuts, low, high):
    def one(dim, parts):
        draws = jax.random.uniform(jax.random.fold_in(jax.random.fold_in(stream_key, 6), dim), (parts,), jnp.float32, low / len(cuts), high / len(cuts))
        return jnp.repeat(jnp.exp(draws), extent[dim] // parts).reshape((-1,) + (1,) * (len(extent) - dim - 1))

    factor_of = one(*cuts[0])
    for cut in cuts[1:]:
        factor_of = factor_of * one(*cut)
    return factor_of


def scatter_about(own_key, extent, deviation, limit, cuts=(), kind=jnp.bfloat16):
    array = jax.random.normal(own_key, extent, jnp.float32) * deviation
    if len(cuts) > 0:
        array = steps_of(own_key, extent, cuts, -0.22, 0.18) * array
    return jnp.clip(array, min=-limit, max=limit).astype(kind)


def bell_draw_with(own_key, dims, scale, bound, shards, heavy, held_as=jnp.bfloat16):
    array = scale * jax.random.normal(own_key, dims, jnp.float32)
    if shards:
        array = array * steps_of(own_key, dims, shards, -0.22, 0.18)
    return jnp.clip(with_spikes(array, jax.random.fold_in(own_key, 3), *heavy), -bound, bound).astype(held_as)


def setup_inputs(seed: int = 0) -> dict:
    key_list = jax.random.split(jax.random.key(seed), 8)
    tokens = bell_draw_with(key_list[0], (TOKENS, D), 1.0, 6.0, ((0, 16), (1, 16)), (0, 1, 16, 2.0))
    cotangent = bell_draw_with(key_list[1], (TOKENS, D), 1.0, 6.0, ((0, 16), (1, 16)), (0, 1, 16, 2.0))
    route_probs = jnp.clip(jnp.exp(math.log(1.0) - 1.609438 * jax.random.uniform(key_list[2], (TOKENS,), jnp.float32) ** steps_of(key_list[2], (TOKENS,), ((0, 16),), -0.2, 0.2)), 0.2, 1.0)
    w_gate = scatter_about(key_list[3], (EXP, D, FF), D ** -0.5, 0.125, ((1, 16), (2, 16)))
    w_up = scatter_about(key_list[4], (EXP, D, FF), D ** -0.5, 0.125, ((1, 16), (2, 16)))
    w_down = scatter_about(key_list[5], (EXP, FF, D), FF ** -0.5, 0.0625, ((1, 16), (2, 16)))
    tile_counts = draw_tile_counts(jax.random.fold_in(key_list[7], 71), 0)
    return {"tokens": tokens, "cotangent": cotangent, "route_probs": route_probs, "w_gate": w_gate, "w_up": w_up, "w_down": w_down, "tile_counts": tile_counts}


def expert_of_slots(tile_counts):
    tile_ends = jnp.cumsum(tile_counts, axis=1).astype(jnp.int32)
    position = jnp.arange(TILES_DEV, dtype=jnp.int32)
    return jnp.sum((position[None, :, None] >= tile_ends[:, None, :]).astype(jnp.int32), axis=2).astype(jnp.int32)


def reference(tokens, cotangent, route_probs, w_gate, w_up, w_down, tile_counts):
    hidden_dev = FF // N_SHARD
    slot_experts = expert_of_slots(tile_counts)
    token_tiles = tokens.reshape(N_DP, TILES_DEV, TILE, D)
    cot_tiles = cotangent.reshape(N_DP, TILES_DEV, TILE, D)
    prob_tiles = route_probs.reshape(N_DP, TILES_DEV, TILE)

    def tile_step(carried, element):
        gate_total, up_total, down_total = carried
        token_tile, cot_tile, prob_tile, raw_expert = element
        is_live = raw_expert < EXP
        expert = jnp.minimum(raw_expert, EXP - 1)
        gate_mat = w_gate[expert]
        up_mat = w_up[expert]
        down_mat = w_down[expert]
        gate_pre = jnp.dot(token_tile, gate_mat, preferred_element_type=jnp.float32)
        up_pre = jnp.dot(token_tile, up_mat, preferred_element_type=jnp.float32)
        gate_sig = jax.nn.sigmoid(gate_pre)
        activated = gate_pre * gate_sig
        hidden = (activated * up_pre).astype(jnp.bfloat16)
        shard_parts = jnp.einsum("tsf,sfd->std", hidden.reshape(TILE, N_SHARD, hidden_dev).astype(jnp.float32),
                                 down_mat.reshape(N_SHARD, hidden_dev, D).astype(jnp.float32))
        rounded = lax.optimization_barrier(shard_parts.astype(jnp.bfloat16))
        ffn_out = jnp.sum(rounded.astype(jnp.float32), axis=0)
        ffn_out = jnp.where(is_live, ffn_out, jnp.zeros_like(ffn_out))
        out_tile = (prob_tile[:, None] * ffn_out).astype(jnp.bfloat16)
        prob_tile_grad = jnp.sum(cot_tile.astype(jnp.float32) * ffn_out, axis=1)
        scaled_f = prob_tile[:, None] * cot_tile.astype(jnp.float32)
        scaled = jnp.where(is_live, scaled_f, jnp.zeros_like(scaled_f)).astype(jnp.bfloat16)
        hidden_grad = jnp.dot(scaled, down_mat.T, preferred_element_type=jnp.float32)
        pre_gate_grad = (hidden_grad * up_pre * gate_sig * (1.0 + gate_pre * (1.0 - gate_sig))).astype(jnp.bfloat16)
        pre_up_grad = (hidden_grad * activated).astype(jnp.bfloat16)
        input_parts = jnp.einsum("tsf,dsf->std", pre_gate_grad.reshape(TILE, N_SHARD, hidden_dev).astype(jnp.float32),
                                 gate_mat.reshape(D, N_SHARD, hidden_dev).astype(jnp.float32))
        input_parts = input_parts + jnp.einsum("tsf,dsf->std", pre_up_grad.reshape(TILE, N_SHARD, hidden_dev).astype(jnp.float32),
                                               up_mat.reshape(D, N_SHARD, hidden_dev).astype(jnp.float32))
        rounded_in = lax.optimization_barrier(input_parts.astype(jnp.bfloat16))
        input_tile = jnp.sum(rounded_in.astype(jnp.float32), axis=0).astype(jnp.bfloat16)
        gate_total = gate_total.at[expert].add(jnp.dot(token_tile.T, pre_gate_grad, preferred_element_type=jnp.float32))
        up_total = up_total.at[expert].add(jnp.dot(token_tile.T, pre_up_grad, preferred_element_type=jnp.float32))
        down_total = down_total.at[expert].add(jnp.dot(hidden.T, scaled, preferred_element_type=jnp.float32))
        return (gate_total, up_total, down_total), (out_tile, prob_tile_grad, input_tile)

    def group_step(totals, element):
        start_state = (jnp.zeros((EXP, D, FF), jnp.float32), jnp.zeros((EXP, D, FF), jnp.float32),
                       jnp.zeros((EXP, FF, D), jnp.float32))
        group_sums, results = lax.scan(tile_step, start_state, element)
        new_totals = []
        for running, group_sum in zip(totals, group_sums):
            rounded_sum = lax.optimization_barrier(group_sum.astype(jnp.bfloat16))
            new_totals.append(running + rounded_sum.astype(jnp.float32))
        return tuple(new_totals), results

    first = (jnp.zeros((EXP, D, FF), jnp.float32), jnp.zeros((EXP, D, FF), jnp.float32),
             jnp.zeros((EXP, FF, D), jnp.float32))
    totals, (out_tiles, prob_grads, input_tiles) = lax.scan(group_step, first,
                                                            (token_tiles, cot_tiles, prob_tiles, slot_experts))
    layer_out = out_tiles.reshape(TOKENS, D)
    prob_grad = prob_grads.reshape(TOKENS)
    input_grad = input_tiles.reshape(TOKENS, D)
    return (layer_out, prob_grad, input_grad, totals[0].astype(jnp.bfloat16),
            totals[1].astype(jnp.bfloat16), totals[2].astype(jnp.bfloat16))
```

```python
import jax
import jax.numpy as jnp
from jax import lax
from jax.sharding import Mesh, PartitionSpec as P

TILE = 128
F32 = jnp.float32
BF16 = jnp.bfloat16
SIZES = {"zh": 4, "y": 4, "x": 4, "zl": 2, "c": 2}


def shift(v, axis, by):
    n = SIZES[axis]
    return lax.ppermute(v, axis, [(i, (i + by) % n) for i in range(n)])


def put(buf, v, index, dim):
    return lax.dynamic_update_slice_in_dim(buf, v, index, dim)


def pick(v, index):
    return lax.dynamic_index_in_dim(v, index, 0, keepdims=False)


def pair_stack(v, other, axis):
    i = lax.axis_index(axis)
    buf = jnp.zeros((2,) + v.shape, v.dtype)
    return put(put(buf, v[None], i, 0), other[None], 1 - i, 0)


def ring_gather(v, axis, dim):
    i = lax.axis_index(axis)
    width = v.shape[dim]
    half = v.shape[0] // 2
    left = shift(v, axis, 1)
    right = shift(v, axis, 3)
    far_a = shift(left[:half], axis, 1)
    far_b = shift(right[half:], axis, 3)
    shape = list(v.shape)
    shape[dim] = 4 * width
    buf = jnp.zeros(shape, v.dtype)

    def at(k):
        return lax.rem(i + k, 4) * width

    buf = put(buf, v, at(0), dim)
    buf = put(buf, left, at(3), dim)
    buf = put(buf, right, at(1), dim)
    far = jnp.concatenate([far_a, far_b], axis=0)
    return put(buf, far, at(2), dim)


def gather_groups(v):
    i = lax.axis_index("zh")
    buf = jnp.zeros((4,) + v.shape, v.dtype)
    buf = put(buf, v[None], i, 0)
    for k in (1, 3, 2):
        buf = put(buf, shift(v, "zh", k)[None], lax.rem(i + 4 - k, 4), 0)
    return buf


def gather_rows(v):
    c = lax.axis_index("c")
    groups = gather_groups(v)
    mine = lax.dynamic_slice_in_dim(groups, 2 * c, 2, 0)
    theirs = lax.dynamic_slice_in_dim(groups, 2 * (1 - c), 2, 0)
    both = pair_stack(mine, shift(theirs, "c", 1), "c")
    four = pair_stack(both, shift(both, "zl", 1), "zl")
    rows = four.transpose(2, 3, 0, 1, 4).reshape(768, 512)
    return ring_gather(rows, "x", 1)


def scatter_rows(part):
    zh, zl, c = (lax.axis_index(a) for a in ("zh", "zl", "c"))
    blocks = part.reshape(768, 4, 512).transpose(1, 0, 2)
    got = lax.all_to_all(blocks, "x", 0, 0)
    v = jnp.sum(got.astype(F32), axis=0).astype(BF16)
    v = v.reshape(2, 384, 2, 2, 128).transpose(2, 3, 0, 1, 4)
    kept = pick(v, zl).astype(F32) + shift(pick(v, 1 - zl), "zl", 1).astype(F32)
    v = kept.astype(BF16)
    mine, theirs = pick(v, c), shift(pick(v, 1 - c), "c", 1)
    four = jnp.zeros((4, 384, 128), BF16)
    four = put(put(four, mine, 2 * c, 0), theirs, 2 * (1 - c), 0)
    total = pick(four, zh).astype(F32)
    for k in (1, 3, 2):
        total = total + shift(pick(four, lax.rem(zh + k, 4)), "zh", k).astype(F32)
    return total


def gather_weights(w_gate, w_up, w_down):
    g = w_gate.reshape(2, 128, 4, 128).transpose(2, 0, 1, 3)
    u = w_up.reshape(2, 128, 4, 128).transpose(2, 0, 1, 3)
    d = w_down.reshape(2, 4, 128, 128).transpose(1, 0, 2, 3)
    packed = jnp.stack([g, u, d], axis=2)
    mine = lax.all_to_all(packed, "zh", 0, 0)
    own = ring_weights(mine)
    other = shift(own, "c", 1)
    both = jnp.stack([own, other])
    wgu = both[:, :, :, :, :2].transpose(2, 1, 5, 3, 4, 0, 6).reshape(2048, 1024)
    wd = both[:, :, :, :, 2].transpose(3, 0, 4, 2, 1, 5).reshape(512, 2048)
    return wgu, wd


def ring_weights(mine):
    i = lax.axis_index("y")
    left = shift(mine, "y", 1)
    right = shift(mine, "y", 3)
    far = jnp.concatenate([shift(left[:2], "y", 1), shift(right[2:], "y", 3)], axis=0)
    buf = jnp.zeros((4,) + mine.shape, mine.dtype)
    for k, v in ((0, mine), (3, left), (1, right), (2, far)):
        buf = put(buf, v[None], lax.rem(i + k, 4), 0)
    return buf


def scatter_weights(dgu, dd):
    a = dgu.reshape(4, 4, 128, 2, 2, 2, 128).transpose(5, 1, 0, 3, 4, 2, 6)
    b = dd.reshape(2, 2, 128, 4, 4, 128).transpose(1, 4, 3, 0, 2, 5)
    packed = jnp.concatenate([a, b[:, :, :, :, None]], axis=4)
    v = (packed[0].astype(F32) + shift(packed[1], "c", 1).astype(F32)).astype(BF16)
    v = lax.all_to_all(v, "y", 0, 0)
    v = jnp.sum(v.astype(F32), axis=0).astype(BF16)
    v = lax.all_to_all(v, "zh", 0, 0)
    gate = v[:, :, 0].transpose(1, 2, 0, 3).reshape(2, 128, 512)
    up = v[:, :, 1].transpose(1, 2, 0, 3).reshape(2, 128, 512)
    down = v[:, :, 2].transpose(1, 0, 2, 3).reshape(2, 512, 128)
    return gate, up, down


def shard_sum(v):
    v = v + shift(v, "c", 1)
    v = v + shift(v, "zl", 1)
    return v + shift(v, "x", 1) + shift(v, "x", 3) + shift(v, "x", 2)


def dot(a, b, dims):
    return lax.dot_general(a, b, (dims, ((), ())), preferred_element_type=F32)


def per_device(tokens, cotangent, route_probs, w_gate, w_up, w_down, tile_counts):
    c = lax.axis_index("c")
    cot = cotangent.astype(F32)
    scaled = (route_probs[:, None] * cot).astype(BF16)
    counts = lax.dynamic_slice_in_dim(gather_groups(tile_counts[0]), 2 * c, 2, 0)
    wgu, wd = gather_weights(w_gate, w_up, w_down)
    x = gather_rows(tokens)
    s = gather_rows(scaled)

    slot = jnp.arange(384, dtype=jnp.int32) // TILE
    first = counts[:, :1]
    last = first + counts[:, 1:]
    is_a = (slot[None] < first).reshape(768, 1)
    is_b = ((slot[None] >= first) & (slot[None] < last)).reshape(768, 1)

    pre = dot(x, wgu, ((1,), (0,))).reshape(768, 2, 2, 256)
    gate_pre = jnp.where(is_a, pre[:, 0, 0], pre[:, 1, 0])
    up_pre = jnp.where(is_a, pre[:, 0, 1], pre[:, 1, 1])
    sig = jax.nn.sigmoid(gate_pre)
    act = gate_pre * sig
    hidden = (act * up_pre).astype(BF16)
    zero = jnp.zeros((), BF16)

    def by_expert(v):
        return [jnp.where(is_a, v, zero), jnp.where(is_b, v, zero)]

    hid = jnp.concatenate(by_expert(hidden), axis=1)
    part_out = dot(hid, wd, ((1,), (0,))).astype(BF16)
    hg = dot(s, wd, ((1,), (1,))).reshape(768, 2, 256)
    hg = jnp.where(is_a, hg[:, 0], hg[:, 1])
    pg = (hg * up_pre * sig * (1.0 + gate_pre * (1.0 - sig))).astype(BF16)
    pu = (hg * act).astype(BF16)
    pga, pgb = by_expert(pg)
    pua, pub = by_expert(pu)
    pre_grad = jnp.concatenate([pga, pua, pgb, pub], axis=1)
    part_in = dot(pre_grad, wgu, ((1,), (1,))).astype(BF16)
    dgu = dot(x, pre_grad, ((0,), (0,))).astype(BF16)
    dd = dot(hid, s, ((0,), (0,))).astype(BF16)

    ffn_out = scatter_rows(part_out)
    input_grad = scatter_rows(part_in).astype(BF16)
    gate_grad, up_grad, down_grad = scatter_weights(dgu, dd)
    layer_out = (route_probs[:, None] * ffn_out).astype(BF16)
    prob_grad = shard_sum(jnp.sum(cot * ffn_out, axis=1))
    return layer_out, prob_grad, input_grad, gate_grad, up_grad, down_grad


def solution(mesh):
    fine = Mesh(mesh.devices.reshape(4, 4, 4, 2, 2), tuple(SIZES))
    dp, shard = ("zh", "y"), ("x", "zl", "c")
    rows, cols, both = P(dp, shard), P(None, dp, shard), P(None, shard, dp)
    return jax.shard_map(
        per_device,
        mesh=fine,
        in_specs=(rows, rows, P(dp), cols, cols, both, P(dp, None)),
        out_specs=(rows, P(dp), rows, cols, cols, both),
        check_vma=False,
    )
```

```python
import jax
import jax.numpy as jnp
from jax import lax
from jax.experimental import pallas as pl
from jax.experimental.pallas import tpu as pltpu
from jax.sharding import Mesh, PartitionSpec as P

TILE = 128
ROWS = 384
F32 = jnp.float32
BF16 = jnp.bfloat16
SIZES = {"zh": 4, "y": 4, "x": 4, "zl": 2, "c": 2}
VMEM = pl.BlockSpec(memory_space=pltpu.VMEM)
SMEM = pl.BlockSpec(memory_space=pltpu.SMEM)


def call(kernel, outs, n_smem, args, scratch=(), deps=(), flops=0, nbytes=0):
    n, m = len(args), len(deps)

    def body(*refs):
        kernel(*refs[:n], *refs[n + m :])

    return pl.pallas_call(
        body,
        out_shape=[jax.ShapeDtypeStruct(s, d) for s, d in outs],
        in_specs=[SMEM] * n_smem
        + [VMEM] * (n - n_smem)
        + [pl.BlockSpec(memory_space=pl.ANY)] * m,
        out_specs=[VMEM] * len(outs),
        scratch_shapes=list(scratch),
        compiler_params=pltpu.CompilerParams(vmem_limit_bytes=56 * 2**20),
        cost_estimate=pl.CostEstimate(
            flops=flops, bytes_accessed=nbytes, transcendentals=0
        ),
        name=kernel.__name__,
    )(*args, *deps)


def shift(v, axis, by):
    n = SIZES[axis]
    return lax.ppermute(v, axis, [(i, (i + by) % n) for i in range(n)])


def to_core(v, k):
    pairs = []
    for zh in range(4):
        for c in range(2):
            a, b = divmod(zh, 2)
            pairs.append((zh * 2 + c, ((2 * b + c + k) % 4) * 2 + a))
    return lax.ppermute(v, ("zh", "c"), pairs)


def from_core(v, k):
    pairs = []
    for zh in range(4):
        for c in range(2):
            a, b = divmod(zh, 2)
            pairs.append((((2 * b + c + k) % 4) * 2 + a, zh * 2 + c))
    return lax.ppermute(v, ("zh", "c"), pairs)


def ring(v, axis):
    half = v.shape[0] // 2
    before = shift(v, axis, 1)
    after = shift(v, axis, 3)
    return [v, before, after, shift(before[:half], axis, 1), shift(after[half:], axis, 3)]


def mod4(v):
    return lax.rem(v + 4, 4)


def dot(a, b, dims):
    return lax.dot_general(a, b, (dims, ((), ())), preferred_element_type=F32)


def pack_tokens(counts, tok, cot, prob, msg):
    msg[0:ROWS] = tok[...]
    msg[ROWS : 2 * ROWS] = (prob[...] * cot[...].astype(F32)).astype(BF16)
    one = jnp.ones((8, 128), F32)
    tile = jnp.concatenate(
        [one * counts[0, 0].astype(F32), one * counts[0, 1].astype(F32)], axis=0
    )
    msg[2 * ROWS : 2 * ROWS + 16] = tile.astype(BF16)


def pack_weights(pos, wg, wu, wd, w0, w1, w2, w3):
    for k, out in enumerate((w0, w1, w2, w3)):
        q = pl.multiple_of(mod4(pos[0] + k) * 128, 128)
        for e in range(2):
            out[e * 3] = wg[e, :, pl.ds(q, 128)]
            out[e * 3 + 1] = wu[e, :, pl.ds(q, 128)]
            out[e * 3 + 2] = wd[e, pl.ds(q, 128), :]


def place_rows(pos, pieces, base, dst):
    zh, x, zl = pos[0], pos[2], pos[3]
    own, before, after, far_a, far_b = pieces
    for hop, zlrel, ref, lead in (
        (0, 0, own, 0),
        (0, 1, own, 1),
        (3, 0, before, 0),
        (3, 1, before, 1),
        (1, 0, after, 0),
        (1, 1, after, 1),
        (2, 0, far_a, 0),
        (2, 1, far_b, 0),
    ):
        xs = mod4(x + hop)
        zs = lax.rem(zl + zlrel, 2)
        for k in range(4):
            s = mod4(zh - k)
            b, cs = lax.div(s, 2), lax.rem(s, 2)
            col = pl.multiple_of((xs * 4 + zs * 2 + cs) * 128, 128)
            row = pl.multiple_of(b * ROWS, 128)
            at = (lead * 4 + k) * (2 * ROWS + 16) + base
            dst[pl.ds(row, ROWS), pl.ds(col, 128)] = ref[at : at + ROWS, :]


def place_weights(pos, own, other, wgu, wd):
    zh, y = pos[0], pos[1]
    for cs, pieces in enumerate((own, other)):
        a, before, after, far_a, far_b = pieces
        for hop, ref, ks in (
            (0, a, range(4)),
            (3, before, range(4)),
            (1, after, range(4)),
            (2, far_a, range(2)),
            (2, far_b, range(2, 4)),
        ):
            for i, k in enumerate(ks):
                d = pl.multiple_of((mod4(zh - k) * 4 + mod4(y + hop)) * 128, 128)
                for e in range(2):
                    for m in range(2):
                        col = (e * 4 + m * 2 + cs) * 128
                        wgu[pl.ds(d, 128), col : col + 128] = ref[i, e * 3 + m]
                    row = (e * 2 + cs) * 128
                    wd[row : row + 128, pl.ds(d, 128)] = ref[i, e * 3 + 2]


def forward_kernel(*refs):
    pos, cnt, x = refs[:3]
    wo, wx = refs[3:8], refs[8:13]
    wgu, wd, gate_out, up_out, mask, hid, part = refs[13:]
    place_weights(pos, wo, wx, wgu, wd)
    slot = (lax.broadcasted_iota(jnp.int32, (ROWS, 128), 0) // TILE).astype(F32)
    for k in (0, 1, 2, 3):
        b = lax.div(mod4(pos[0] - k), 2)
        row = pl.multiple_of(b * ROWS, 128)
        tile = cnt[k * 16 : k * 16 + 16, :].astype(F32)
        first = tile[0:1, :]
        last = first + tile[8:9, :]
        mask[0, pl.ds(row, ROWS), :] = jnp.where(slot < first, 1.0, 0.0)
        mask[1, pl.ds(row, ROWS), :] = jnp.where((slot >= first) & (slot < last), 1.0, 0.0)

    @pl.loop(0, 3)
    def _(r):
        at = pl.multiple_of(r * 256, 256)
        rows = pl.ds(at, 256)
        pre = dot(x[rows, :], wgu[...], ((1,), (0,)))
        ma, mb = mask[0, rows, :], mask[1, rows, :]
        is_a = jnp.concatenate([ma, ma], axis=1) > 0.5
        is_b = jnp.concatenate([mb, mb], axis=1) > 0.5
        gate = jnp.where(is_a, pre[:, 0:256], pre[:, 512:768])
        up = jnp.where(is_a, pre[:, 256:512], pre[:, 768:1024])
        gate_out[rows, :] = gate
        up_out[rows, :] = up
        h = gate * jax.nn.sigmoid(gate) * up
        zero = jnp.zeros_like(h)
        hid[rows, 0:256] = jnp.where(is_a, h, zero).astype(BF16)
        hid[rows, 256:512] = jnp.where(is_b, h, zero).astype(BF16)
        for xs in range(4):
            part[xs, rows, :] = dot(
                hid[rows, :], wd[:, xs * 512 : (xs + 1) * 512], ((1,), (0,))
            ).astype(BF16)


def place_tokens(pos, own, before, after, far_a, far_b, x):
    place_rows(pos, (own, before, after, far_a, far_b), 0, x)


def backward_kernel(*refs):
    pos, sp = refs[0], refs[1:6]
    x, wgu, wd, gate_in, up_in, mask, hid = refs[6:13]
    part, d_own, d_other, s, grad, dots = refs[13:]
    dots[...] = jnp.zeros_like(dots)
    place_rows(pos, sp, ROWS, s)

    @pl.loop(0, 3)
    def _(r):
        at = pl.multiple_of(r * 256, 256)
        rows = pl.ds(at, 256)
        both = dot(s[rows, :], wd[...], ((1,), (1,)))
        ma, mb = mask[0, rows, :], mask[1, rows, :]
        is_a = jnp.concatenate([ma, ma], axis=1) > 0.5
        is_b = jnp.concatenate([mb, mb], axis=1) > 0.5
        hg = jnp.where(is_a, both[:, 0:256], both[:, 256:512])
        gate, up = gate_in[rows, :], up_in[rows, :]
        sig = jax.nn.sigmoid(gate)
        pg = hg * up * sig * (1.0 + gate * (1.0 - sig))
        pu = hg * (gate * sig)
        zero = jnp.zeros_like(pg)
        prod = hg * (hid[rows, 0:256].astype(F32) + hid[rows, 256:512].astype(F32))
        sums = lax.dot_general(
            jnp.ones((8, 256), F32),
            prod,
            (((1,), (1,)), ((), ())),
            precision=lax.Precision.HIGHEST,
            preferred_element_type=F32,
        )
        for i in range(2):
            dots[pl.ds(r * 2 + i, 1), :] = sums[0:1, i * 128 : (i + 1) * 128]
        grad[rows, 0:256] = jnp.where(is_a, pg, zero).astype(BF16)
        grad[rows, 256:512] = jnp.where(is_a, pu, zero).astype(BF16)
        grad[rows, 512:768] = jnp.where(is_b, pg, zero).astype(BF16)
        grad[rows, 768:1024] = jnp.where(is_b, pu, zero).astype(BF16)
        for xs in range(4):
            part[xs, rows, :] = dot(
                grad[rows, :], wgu[xs * 512 : (xs + 1) * 512, :], ((1,), (1,))
            ).astype(BF16)

    tile = dots[...].astype(BF16)
    for xs in range(4):
        for i in range(4):
            part[xs, 768:784, i * 128 : (i + 1) * 128] = tile

    dests = (d_own, d_other)

    @pl.loop(0, 4)
    def _(z):
        cols = pl.ds(pl.multiple_of(z * 512, 512), 512)
        dgu = dot(x[:, cols], grad[...], ((0,), (0,))).astype(BF16)
        dd = dot(hid[...], s[:, cols], ((0,), (0,))).astype(BF16)
        for cs in range(2):
            for y in range(4):
                yk, zk = mod4(y - pos[1]), mod4(z - pos[0])
                for e in range(2):
                    for m in range(2):
                        col = (e * 4 + m * 2 + cs) * 128
                        dests[cs][yk, zk, e * 3 + m] = dgu[
                            y * 128 : (y + 1) * 128, col : col + 128
                        ]
                    row = (e * 2 + cs) * 128
                    dests[cs][yk, zk, e * 3 + 2] = dd[
                        row : row + 128, y * 128 : (y + 1) * 128
                    ]


def sum_x_kernel(pos, got, keep, send):
    zl = pos[3]
    for out, at in ((send, (1 - zl) * 256), (keep, zl * 256)):
        cols = pl.ds(pl.multiple_of(at, 128), 256)
        total = got[0, :, cols].astype(F32)
        for i in (1, 2, 3):
            total = total + got[i, :, cols].astype(F32)
        out[...] = total.astype(out.dtype)


def split_kernel(pos, keep, got, o0, o1, o2, o3, tmp):
    tmp[...] = keep[...] + got[...].astype(F32)
    for k, out in enumerate((o0, o1, o2, o3)):
        s = mod4(pos[0] - k)
        row = pl.multiple_of(lax.div(s, 2) * ROWS, 128)
        col = pl.multiple_of(lax.rem(s, 2) * 128, 128)
        out[0:ROWS] = tmp[pl.ds(row, ROWS), pl.ds(col, 128)].astype(BF16)
        if out.shape[0] > ROWS:
            out[ROWS:] = tmp[2 * ROWS :, pl.ds(col, 128)].astype(BF16)


def finish_kernel(pos, p0, p1, p2, p3, gate, up, down):
    for k, ref in enumerate((p0, p1, p2, p3)):
        q = pl.multiple_of(mod4(pos[0] - k) * 128, 128)
        for e in range(2):
            gate[e, :, pl.ds(q, 128)] = ref[e * 3]
            up[e, :, pl.ds(q, 128)] = ref[e * 3 + 1]
            down[e, pl.ds(q, 128), :] = ref[e * 3 + 2]


def add_cores_kernel(a, b, o0, o1, o2, o3):
    for k, out in enumerate((o0, o1, o2, o3)):
        out[...] = (a[k].astype(F32) + b[k].astype(F32)).astype(BF16)


def sum_y_kernel(a, b, c, d, o0, o1, o2, o3):
    for k, out in enumerate((o0, o1, o2, o3)):
        total = a[k].astype(F32) + b[k].astype(F32) + c[k].astype(F32) + d[k].astype(F32)
        out[...] = total.astype(BF16)


def exchange(parts, axis):
    return [parts[0]] + [shift(parts[k], axis, k) for k in (1, 2, 3)]


def scatter_rows(pos, part, deps=(), split_deps=()):
    rows = part.shape[1]
    extra = rows - 2 * ROWS
    keep, send = call(
        sum_x_kernel,
        [((rows, 256), F32), ((rows, 256), BF16)],
        1,
        [pos, lax.all_to_all(part, "x", 0, 0)],
        deps=deps,
    )
    blocks = call(
        split_kernel,
        [((ROWS + extra, 128), BF16)] * 4,
        1,
        [pos, keep, shift(send, "zl", 1)],
        [pltpu.VMEM((rows, 256), F32)],
        deps=split_deps,
    )
    terms = [from_core(b, k).astype(F32) for k, b in enumerate(blocks)]
    return terms[0] + terms[1] + terms[2] + terms[3]


def add_cores(d_own, d_other):
    return call(
        add_cores_kernel,
        [((4, 6, 128, 128), BF16)] * 4,
        0,
        [d_own, shift(d_other, "c", 1)],
    )


def per_device(tokens, cotangent, route_probs, w_gate, w_up, w_down, tile_counts):
    pos = jnp.stack([lax.axis_index(a) for a in SIZES]).astype(jnp.int32)
    (msg,) = call(
        pack_tokens,
        [((2 * ROWS + 16, 128), BF16)],
        1,
        [tile_counts, tokens, cotangent, route_probs[:, None]],
    )
    got = [to_core(msg, k) for k in range(4)]
    cnt = jnp.concatenate([g[2 * ROWS :] for g in got])
    ts = jnp.concatenate(got)
    ts_ring = ring(jnp.concatenate([ts, shift(ts, "zl", 1)]), "x")
    w = call(
        pack_weights,
        [((6, 128, 128), BF16)] * 4,
        1,
        [pos, w_gate, w_up, w_down],
    )
    own = ring(jnp.stack(exchange(w, "zh")), "y")
    other = [shift(v, "c", 1) for v in own]
    (x,) = call(place_tokens, [((768, 2048), BF16)], 1, [pos, *ts_ring])

    wgu, wd, gate, up, mask, hid, part_out = call(
        forward_kernel,
        [
            ((2048, 1024), BF16),
            ((512, 2048), BF16),
            ((768, 256), F32),
            ((768, 256), F32),
            ((2, 768, 128), F32),
            ((768, 512), BF16),
            ((4, 768, 512), BF16),
        ],
        1,
        [pos, cnt, x, *own, *other],
        flops=2 * 768 * 2048 * 1536,
        nbytes=30 << 20,
    )
    part_in, d_own, d_other = call(
        backward_kernel,
        [((4, 784, 512), BF16)] + [((4, 4, 6, 128, 128), BF16)] * 2,
        1,
        [pos, *ts_ring, x, wgu, wd, gate, up, mask, hid],
        [
            pltpu.VMEM((768, 2048), BF16),
            pltpu.VMEM((768, 1024), BF16),
            pltpu.VMEM((16, 128), F32),
        ],
        flops=2 * 768 * 2048 * 3072,
        nbytes=30 << 20,
    )
    four = add_cores(d_own, d_other)
    ffn_out = scatter_rows(pos, part_out, deps=four[:1])
    layer_out = (route_probs[:, None] * ffn_out).astype(BF16)
    four = call(sum_y_kernel, [((6, 128, 128), BF16)] * 4, 0, exchange(four, "y"))
    back = scatter_rows(pos, part_in, deps=[layer_out], split_deps=four[:1])
    gate_grad, up_grad, down_grad = call(
        finish_kernel,
        [((2, 128, 512), BF16), ((2, 128, 512), BF16), ((2, 512, 128), BF16)],
        1,
        [pos, *exchange(four, "zh")],
    )
    input_grad = back[:ROWS].astype(BF16)
    row = ROWS + 3 * lax.rem(lax.axis_index("zh"), 2)
    prob_grad = lax.dynamic_slice_in_dim(back, row, 3, 0).reshape(ROWS) / route_probs
    return layer_out, prob_grad, input_grad, gate_grad, up_grad, down_grad


def solution(mesh):
    fine = Mesh(mesh.devices.reshape(4, 4, 4, 2, 2), tuple(SIZES))
    dp, shard = ("zh", "y"), ("x", "zl", "c")
    rows, cols, both = P(dp, shard), P(None, dp, shard), P(None, shard, dp)
    return jax.shard_map(
        per_device,
        mesh=fine,
        in_specs=(rows, rows, P(dp), cols, cols, both, P(dp, None)),
        out_specs=(rows, P(dp), rows, cols, cols, both),
        check_vma=False,
    )
```

```python
import jax
import jax.numpy as jnp
from jax import lax
from jax.experimental import pallas as pl
from jax.experimental.pallas import tpu as pltpu
from jax.sharding import Mesh, PartitionSpec as P

TILE = 128
ROWS = 384
F32 = jnp.float32
BF16 = jnp.bfloat16
SIZES = {"zh": 4, "y": 4, "x": 4, "zl": 2, "c": 2}
VMEM = pl.BlockSpec(memory_space=pltpu.VMEM)
SMEM = pl.BlockSpec(memory_space=pltpu.SMEM)


def call(kernel, outs, n_smem, args, scratch=(), deps=(), flops=0, nbytes=0):
    n, m = len(args), len(deps)

    def body(*refs):
        kernel(*refs[:n], *refs[n + m :])

    return pl.pallas_call(
        body,
        out_shape=[jax.ShapeDtypeStruct(s, d) for s, d in outs],
        in_specs=[SMEM] * n_smem
        + [VMEM] * (n - n_smem)
        + [pl.BlockSpec(memory_space=pl.ANY)] * m,
        out_specs=[VMEM] * len(outs),
        scratch_shapes=list(scratch),
        compiler_params=pltpu.CompilerParams(vmem_limit_bytes=56 * 2**20),
        cost_estimate=pl.CostEstimate(
            flops=flops, bytes_accessed=nbytes, transcendentals=0
        ),
        name=kernel.__name__,
    )(*args, *deps)


def shift(v, axis, by):
    n = SIZES[axis]
    return lax.ppermute(v, axis, [(i, (i + by) % n) for i in range(n)])


def to_far_side(v):
    pairs = []
    for zh in range(4):
        pairs.append((zh * 2, (zh + 3) % 4 * 2 + 1))
        pairs.append((zh * 2 + 1, (zh + 1) % 4 * 2))
    return lax.ppermute(v, ("zh", "zl"), pairs)


def to_core(v, k):
    pairs = []
    for zh in range(4):
        for c in range(2):
            a, b = divmod(zh, 2)
            pairs.append((zh * 2 + c, ((2 * b + c + k) % 4) * 2 + a))
    return lax.ppermute(v, ("zh", "c"), pairs)


def from_core(v, k):
    pairs = []
    for zh in range(4):
        for c in range(2):
            a, b = divmod(zh, 2)
            pairs.append((((2 * b + c + k) % 4) * 2 + a, zh * 2 + c))
    return lax.ppermute(v, ("zh", "c"), pairs)


def ring(v, axis):
    half = v.shape[0] // 2
    before = shift(v, axis, 1)
    after = shift(v, axis, 3)
    return [v, before, after, shift(before[:half], axis, 1), shift(after[half:], axis, 3)]


def mod4(v):
    return lax.rem(v + 4, 4)


def dot(a, b, dims):
    return lax.dot_general(a, b, (dims, ((), ())), preferred_element_type=F32)


def pack_tokens(counts, tok, cot, prob, msg):
    msg[0:ROWS] = tok[...]
    msg[ROWS : 2 * ROWS] = (prob[...] * cot[...].astype(F32)).astype(BF16)
    one = jnp.ones((8, 128), F32)
    tile = jnp.concatenate(
        [one * counts[0, 0].astype(F32), one * counts[0, 1].astype(F32)], axis=0
    )
    msg[2 * ROWS : 2 * ROWS + 16] = tile.astype(BF16)


def pack_weights(pos, wg, wu, wd, w0, w1, w2, w3):
    for k, out in enumerate((w0, w1, w2, w3)):
        q = pl.multiple_of(mod4(pos[0] + k) * 128, 128)
        for e in range(2):
            out[e * 3] = wg[e, :, pl.ds(q, 128)]
            out[e * 3 + 1] = wu[e, :, pl.ds(q, 128)]
            out[e * 3 + 2] = wd[e, pl.ds(q, 128), :]


def place_rows(pos, pieces, base, dst):
    zh, x, zl = pos[0], pos[2], pos[3]
    own, before, after, far_a, far_b = pieces
    for hop, zlrel, ref, lead in (
        (0, 0, own, 0),
        (0, 1, own, 1),
        (3, 0, before, 0),
        (3, 1, before, 1),
        (1, 0, after, 0),
        (1, 1, after, 1),
        (2, 0, far_a, 0),
        (2, 1, far_b, 0),
    ):
        xs = mod4(x + hop)
        zs = lax.rem(zl + zlrel, 2)
        for k in range(4):
            s = mod4(zh - k)
            b, cs = lax.div(s, 2), lax.rem(s, 2)
            col = pl.multiple_of((xs * 4 + zs * 2 + cs) * 128, 128)
            row = pl.multiple_of(b * ROWS, 128)
            at = (lead * 4 + k) * (2 * ROWS + 16) + base
            dst[pl.ds(row, ROWS), pl.ds(col, 128)] = ref[at : at + ROWS, :]


def place_weights(pos, own, other, wgu, wd):
    zh, y = pos[0], pos[1]
    for cs, pieces in enumerate((own, other)):
        a, before, after, far_a, far_b = pieces
        for hop, ref, ks in (
            (0, a, range(4)),
            (3, before, range(4)),
            (1, after, range(4)),
            (2, far_a, range(2)),
            (2, far_b, range(2, 4)),
        ):
            for i, k in enumerate(ks):
                d = pl.multiple_of((mod4(zh - k) * 4 + mod4(y + hop)) * 128, 128)
                for e in range(2):
                    for m in range(2):
                        col = (e * 4 + m * 2 + cs) * 128
                        wgu[pl.ds(d, 128), col : col + 128] = ref[i, e * 3 + m]
                    row = (e * 2 + cs) * 128
                    wd[row : row + 128, pl.ds(d, 128)] = ref[i, e * 3 + 2]


def forward_kernel(*refs):
    pos, cnt, x = refs[:3]
    wo, wx = refs[3:8], refs[8:13]
    wgu, wd, gate_out, up_out, mask, hid, part = refs[13:]
    place_weights(pos, wo, wx, wgu, wd)
    slot = (lax.broadcasted_iota(jnp.int32, (ROWS, 128), 0) // TILE).astype(F32)
    for k in (0, 1, 2, 3):
        b = lax.div(mod4(pos[0] - k), 2)
        row = pl.multiple_of(b * ROWS, 128)
        tile = cnt[k * 16 : k * 16 + 16, :].astype(F32)
        first = tile[0:1, :]
        last = first + tile[8:9, :]
        mask[0, pl.ds(row, ROWS), :] = jnp.where(slot < first, 1.0, 0.0)
        mask[1, pl.ds(row, ROWS), :] = jnp.where((slot >= first) & (slot < last), 1.0, 0.0)

    @pl.loop(0, 3)
    def _(r):
        at = pl.multiple_of(r * 256, 256)
        rows = pl.ds(at, 256)
        pre = dot(x[rows, :], wgu[...], ((1,), (0,)))
        ma, mb = mask[0, rows, :], mask[1, rows, :]
        is_a = jnp.concatenate([ma, ma], axis=1) > 0.5
        is_b = jnp.concatenate([mb, mb], axis=1) > 0.5
        gate = jnp.where(is_a, pre[:, 0:256], pre[:, 512:768])
        up = jnp.where(is_a, pre[:, 256:512], pre[:, 768:1024])
        gate_out[rows, :] = gate
        up_out[rows, :] = up
        h = gate * jax.nn.sigmoid(gate) * up
        zero = jnp.zeros_like(h)
        hid[rows, 0:256] = jnp.where(is_a, h, zero).astype(BF16)
        hid[rows, 256:512] = jnp.where(is_b, h, zero).astype(BF16)
        for xs in range(4):
            part[xs, rows, :] = dot(
                hid[rows, :], wd[:, xs * 512 : (xs + 1) * 512], ((1,), (0,))
            ).astype(BF16)


def place_tokens(pos, own, before, after, far_a, far_b, x):
    place_rows(pos, (own, before, after, far_a, far_b), 0, x)


def backward_kernel(*refs):
    pos, sp = refs[0], refs[1:6]
    x, wgu, wd, gate_in, up_in, mask, hid = refs[6:13]
    part, d_own, d_other, s, grad, dots = refs[13:]
    dots[...] = jnp.zeros_like(dots)
    place_rows(pos, sp, ROWS, s)

    @pl.loop(0, 3)
    def _(r):
        at = pl.multiple_of(r * 256, 256)
        rows = pl.ds(at, 256)
        both = dot(s[rows, :], wd[...], ((1,), (1,)))
        ma, mb = mask[0, rows, :], mask[1, rows, :]
        is_a = jnp.concatenate([ma, ma], axis=1) > 0.5
        is_b = jnp.concatenate([mb, mb], axis=1) > 0.5
        hg = jnp.where(is_a, both[:, 0:256], both[:, 256:512])
        gate, up = gate_in[rows, :], up_in[rows, :]
        sig = jax.nn.sigmoid(gate)
        pg = hg * up * sig * (1.0 + gate * (1.0 - sig))
        pu = hg * (gate * sig)
        zero = jnp.zeros_like(pg)
        prod = hg * (hid[rows, 0:256].astype(F32) + hid[rows, 256:512].astype(F32))
        sums = lax.dot_general(
            jnp.ones((8, 256), F32),
            prod,
            (((1,), (1,)), ((), ())),
            precision=lax.Precision.HIGHEST,
            preferred_element_type=F32,
        )
        for i in range(2):
            dots[pl.ds(r * 2 + i, 1), :] = sums[0:1, i * 128 : (i + 1) * 128]
        grad[rows, 0:256] = jnp.where(is_a, pg, zero).astype(BF16)
        grad[rows, 256:512] = jnp.where(is_a, pu, zero).astype(BF16)
        grad[rows, 512:768] = jnp.where(is_b, pg, zero).astype(BF16)
        grad[rows, 768:1024] = jnp.where(is_b, pu, zero).astype(BF16)
        for xs in range(4):
            part[xs, rows, :] = dot(
                grad[rows, :], wgu[xs * 512 : (xs + 1) * 512, :], ((1,), (1,))
            ).astype(BF16)

    tile = dots[...].astype(BF16)
    for xs in range(4):
        for i in range(4):
            part[xs, 768:784, i * 128 : (i + 1) * 128] = tile

    dests = (d_own, d_other)

    @pl.loop(0, 4)
    def _(z):
        cols = pl.ds(pl.multiple_of(z * 512, 512), 512)
        dgu = dot(x[:, cols], grad[...], ((0,), (0,))).astype(BF16)
        dd = dot(hid[...], s[:, cols], ((0,), (0,))).astype(BF16)
        for cs in range(2):
            for y in range(4):
                yk, zk = mod4(y - pos[1]), mod4(z - pos[0])
                for e in range(2):
                    for m in range(2):
                        col = (e * 4 + m * 2 + cs) * 128
                        dests[cs][yk, zk, e * 3 + m] = dgu[
                            y * 128 : (y + 1) * 128, col : col + 128
                        ]
                    row = (e * 2 + cs) * 128
                    dests[cs][yk, zk, e * 3 + 2] = dd[
                        row : row + 128, y * 128 : (y + 1) * 128
                    ]


def sum_x_kernel(pos, got, keep, send):
    zl = pos[3]
    for out, at in ((send, (1 - zl) * 256), (keep, zl * 256)):
        cols = pl.ds(pl.multiple_of(at, 128), 256)
        total = got[0, :, cols].astype(F32)
        for i in (1, 2, 3):
            total = total + got[i, :, cols].astype(F32)
        out[...] = total.astype(out.dtype)


def split_kernel(pos, keep, got, o0, o1, o2, o3, tmp):
    tmp[...] = keep[...] + got[...].astype(F32)
    for k, out in enumerate((o0, o1, o2, o3)):
        s = mod4(pos[0] - k)
        row = pl.multiple_of(lax.div(s, 2) * ROWS, 128)
        col = pl.multiple_of(lax.rem(s, 2) * 128, 128)
        out[0:ROWS] = tmp[pl.ds(row, ROWS), pl.ds(col, 128)].astype(BF16)
        if out.shape[0] > ROWS:
            out[ROWS:] = tmp[2 * ROWS :, pl.ds(col, 128)].astype(BF16)


def finish_kernel(pos, p0, p1, p2, p3, gate, up, down):
    for k, ref in enumerate((p0, p1, p2, p3)):
        q = pl.multiple_of(mod4(pos[0] - k) * 128, 128)
        for e in range(2):
            gate[e, :, pl.ds(q, 128)] = ref[e * 3]
            up[e, :, pl.ds(q, 128)] = ref[e * 3 + 1]
            down[e, pl.ds(q, 128), :] = ref[e * 3 + 2]


def add_cores_kernel(a, b, o0, o1, o2, o3):
    for k, out in enumerate((o0, o1, o2, o3)):
        out[...] = (a[k].astype(F32) + b[k].astype(F32)).astype(BF16)


def sum_y_kernel(a, b, c, d, o0, o1, o2, o3):
    for k, out in enumerate((o0, o1, o2, o3)):
        total = a[k].astype(F32) + b[k].astype(F32) + c[k].astype(F32) + d[k].astype(F32)
        out[...] = total.astype(BF16)


def exchange(parts, axis):
    return [parts[0]] + [shift(parts[k], axis, k) for k in (1, 2, 3)]


def scatter_rows(pos, part, deps=(), split_deps=()):
    rows = part.shape[1]
    extra = rows - 2 * ROWS
    keep, send = call(
        sum_x_kernel,
        [((rows, 256), F32), ((rows, 256), BF16)],
        1,
        [pos, lax.all_to_all(part, "x", 0, 0)],
        deps=deps,
    )
    got = jnp.concatenate([shift(send[:ROWS], "zl", 1), to_far_side(send[ROWS:])])
    blocks = call(
        split_kernel,
        [((ROWS + extra, 128), BF16)] * 4,
        1,
        [pos, keep, got],
        [pltpu.VMEM((rows, 256), F32)],
        deps=split_deps,
    )
    terms = [from_core(b, k).astype(F32) for k, b in enumerate(blocks)]
    return terms[0] + terms[1] + terms[2] + terms[3]


def add_cores(d_own, d_other):
    return call(
        add_cores_kernel,
        [((4, 6, 128, 128), BF16)] * 4,
        0,
        [d_own, shift(d_other, "c", 1)],
    )


def per_device(tokens, cotangent, route_probs, w_gate, w_up, w_down, tile_counts):
    pos = jnp.stack([lax.axis_index(a) for a in SIZES]).astype(jnp.int32)
    (msg,) = call(
        pack_tokens,
        [((2 * ROWS + 16, 128), BF16)],
        1,
        [tile_counts, tokens, cotangent, route_probs[:, None]],
    )
    got = [to_core(msg, k) for k in range(4)]
    cnt = jnp.concatenate([g[2 * ROWS :] for g in got])
    ts = jnp.concatenate(got)
    low, high = jnp.concatenate([got[3], got[0]]), jnp.concatenate(got[1:3])
    crossing = jnp.where(lax.axis_index("zl") == 0, low, high)
    partner = shift(jnp.concatenate(got[:2]), "zl", 1)
    ts_ring = ring(jnp.concatenate([ts, partner, to_far_side(crossing)]), "x")
    w = call(
        pack_weights,
        [((6, 128, 128), BF16)] * 4,
        1,
        [pos, w_gate, w_up, w_down],
    )
    own = ring(jnp.stack(exchange(w, "zh")), "y")
    other = [shift(v, "c", 1) for v in own]
    (x,) = call(place_tokens, [((768, 2048), BF16)], 1, [pos, *ts_ring])

    wgu, wd, gate, up, mask, hid, part_out = call(
        forward_kernel,
        [
            ((2048, 1024), BF16),
            ((512, 2048), BF16),
            ((768, 256), F32),
            ((768, 256), F32),
            ((2, 768, 128), F32),
            ((768, 512), BF16),
            ((4, 768, 512), BF16),
        ],
        1,
        [pos, cnt, x, *own, *other],
        flops=2 * 768 * 2048 * 1536,
        nbytes=30 << 20,
    )
    part_in, d_own, d_other = call(
        backward_kernel,
        [((4, 784, 512), BF16)] + [((4, 4, 6, 128, 128), BF16)] * 2,
        1,
        [pos, *ts_ring, x, wgu, wd, gate, up, mask, hid],
        [
            pltpu.VMEM((768, 2048), BF16),
            pltpu.VMEM((768, 1024), BF16),
            pltpu.VMEM((16, 128), F32),
        ],
        flops=2 * 768 * 2048 * 3072,
        nbytes=30 << 20,
    )
    four = add_cores(d_own, d_other)
    ffn_out = scatter_rows(pos, part_out, deps=four[:1])
    layer_out = (route_probs[:, None] * ffn_out).astype(BF16)
    four = call(sum_y_kernel, [((6, 128, 128), BF16)] * 4, 0, exchange(four, "y"))
    back = scatter_rows(pos, part_in, deps=[layer_out], split_deps=four[:1])
    gate_grad, up_grad, down_grad = call(
        finish_kernel,
        [((2, 128, 512), BF16), ((2, 128, 512), BF16), ((2, 512, 128), BF16)],
        1,
        [pos, *exchange(four, "zh")],
    )
    input_grad = back[:ROWS].astype(BF16)
    row = ROWS + 3 * lax.rem(lax.axis_index("zh"), 2)
    prob_grad = lax.dynamic_slice_in_dim(back, row, 3, 0).reshape(ROWS) / route_probs
    return layer_out, prob_grad, input_grad, gate_grad, up_grad, down_grad


def solution(mesh):
    fine = Mesh(mesh.devices.reshape(4, 4, 4, 2, 2), tuple(SIZES))
    dp, shard = ("zh", "y"), ("x", "zl", "c")
    rows, cols, both = P(dp, shard), P(None, dp, shard), P(None, shard, dp)
    return jax.shard_map(
        per_device,
        mesh=fine,
        in_specs=(rows, rows, P(dp), cols, cols, both, P(dp, None)),
        out_specs=(rows, P(dp), rows, cols, cols, both),
        check_vma=False,
    )
```
